32 devices in a mesh: tile: 16 (over z, x, core), dp: 2 (over y).
Axes of the slice: x: 2, y: 2, z: 4, core: 2. Of those that a mesh axis runs over, the one named last changes fastest.
Arguments:
- feature_map: bfloat16 [2, 256, 64, 256], P('dp', 'tile'), may hold values from -6 to 6
- weight: bfloat16 [9, 256, 256], replicated, may hold values from -0.125 to 0.125
- mask_grad: bfloat16 [2, 16, 2, 14, 14, 256], P('dp', 'tile'), may hold values from -6 to 6
- send_count: int32 [2, 16, 2], P('dp', 'tile'), may hold values from 0 to 2, as said below
- send_row: int32 [2, 16, 2, 2], P('dp', 'tile'), may hold values from 0 to 15
- send_col: int32 [2, 16, 2, 2], P('dp', 'tile'), may hold values from 0 to 50
Outputs:
- map_grad: float32 [2, 256, 64, 256], P('dp', 'tile')
- weight_grad: float32 [9, 256, 256], replicated
The draws below stay inside these ranges and needn't reach their ends.
Inputs may be any that keep to these rules, and one draw needn't show every extreme that they name: `send_count`: in every tile column each head receives exactly 2 live slots in all; one owner image sends 2 * 2 crops in all, one sends none, every other one 2, which is which drawn for each column; in every column some count equals 2.
All inputs are finite; a program needn't handle non-finite values.
Results may differ from the reference program's by a relative error of at most 0.004.
Values may be sent and summed in bfloat16 or wider, within the bound.
A program may use at most 64 MiB of HBM per device.

```python
import jax
import jax.numpy as jnp
from jax import lax

C = 256
CROP = 14
TH = 16
TW = 64
BOX_DEV = 2
IMAGES = 2
TILES = 16
MAPH = 256
CAP = 2


def draw_send_count(key, part):
    keys = jax.random.split(key, TILES)
    spread = max(IMAGES - 2, 1)

    def column(column_key):
        key_rank, key_place = jax.random.split(column_key)
        ranking = jax.random.permutation(key_rank, IMAGES)
        placing = jax.random.permutation(key_place, IMAGES)
        order = jnp.arange(IMAGES, dtype=jnp.int32)
        heavy = jnp.clip(2 * BOX_DEV - CAP * order, 0, CAP)
        lighter = BOX_DEV - heavy
        before = jnp.cumsum(lighter) - lighter
        upper = before + lighter
        lanes = order[:, None] - 2
        light_count = (upper[None, :] - lanes + spread - 1) // spread - (before[None, :] - lanes + spread - 1) // spread
        table = jnp.where(order[:, None] == 0, heavy[None, :], jnp.where(order[:, None] == 1, 0, light_count))
        return table[ranking][:, placing]
    tables = jax.vmap(column)(keys)
    return jnp.transpose(tables, (1, 0, 2)).astype(jnp.int32)


def place_ends(result, own_key, low, largest):
    index_at = [jax.random.randint(jax.random.fold_in(own_key, axis), (), 0, length) for axis, length in enumerate(result.shape)]
    longest = result.shape.index(max(result.shape))
    beside = index_at[:longest] + [(index_at[longest] + 1) % result.shape[longest]] + index_at[longest + 1:]
    return result.at[tuple(index_at)].set(low).at[tuple(beside)].set(largest)


def strengthened(drawn, own_key, source, target, parts, factor):
    owner, partner = [(jnp.arange(drawn.shape[axis_at]) // (drawn.shape[axis_at] // parts)).reshape([-1 if axis == axis_at else 1 for axis in range(drawn.ndim)]) for axis_at in (source, target)]
    chosen = jax.random.permutation(own_key, parts)[partner]
    strong = (owner == chosen) | (owner == (partner + parts // 2) % parts)
    return jnp.where(strong, factor * drawn, drawn)


def block_levels(own_key, shape, cuts, least, top_value):
    loudness = 1.0
    for position, shards_of in cuts:
        steps = jax.random.uniform(jax.random.fold_in(jax.random.fold_in(own_key, 6), position), (shards_of,), jnp.float32, least / len(cuts), top_value / len(cuts))
        loudness = loudness * jnp.repeat(jnp.exp(steps), shape[position] // shards_of).reshape((-1,) + (1,) * (len(shape) - 1 - position))
    return loudness


def scatter_about(stream_key, shape, scale, bound, cuts=(), held_as=jnp.bfloat16):
    values = jax.random.normal(stream_key, shape, jnp.float32) * scale
    if len(cuts) > 0:
        values = block_levels(stream_key, shape, cuts, -0.22, 0.18) * values
    return jnp.clip(values, min=-bound, max=bound).astype(held_as)


def heavy_noise(rng, extent, scale, reach, shards, heavy, kind=jnp.bfloat16):
    drawn = scale * jax.random.normal(rng, extent, jnp.float32)
    if shards:
        drawn = drawn * block_levels(rng, extent, shards, -0.22, 0.18)
    return jnp.clip(strengthened(drawn, jax.random.fold_in(rng, 3), *heavy), -reach, reach).astype(kind)


def setup_inputs(seed: int = 0) -> dict:
    key_of = jax.random.split(jax.random.key(seed), 7)
    return {
        "feature_map": heavy_noise(key_of[0], (IMAGES, MAPH, TW, C), 1.0, 6.0, ((0, 2), (1, 16)), (1, 3, 16, 2.0)),
        "weight": scatter_about(key_of[1], (9, C, C), (9 * C) ** -0.5, 0.125),
        "mask_grad": scatter_about(key_of[2], (IMAGES, TILES, BOX_DEV, CROP, CROP, C), 1.0, 6.0, ((0, 2), (1, 16))),
        "send_count": draw_send_count(jax.random.fold_in(key_of[6], 71), 0),
        "send_row": place_ends(jax.random.randint(key_of[4], (IMAGES, TILES, IMAGES, CAP), 0, TH), jax.random.fold_in(key_of[4], 1), 0, TH - 1).astype(jnp.int32),
        "send_col": place_ends(jax.random.randint(key_of[5], (IMAGES, TILES, IMAGES, CAP), 0, TW - CROP + 1), jax.random.fold_in(key_of[5], 1), 0, TW - CROP).astype(jnp.int32),
    }


GELU_SCALE = 0.7978845608
GELU_CUBIC = 0.044715


def gelu_slope(values):
    inner = GELU_SCALE * (values + GELU_CUBIC * values * values * values)
    tangent = jnp.tanh(inner)
    outer = 0.5 * values * (1.0 - tangent * tangent) * GELU_SCALE * (1.0 + 3.0 * GELU_CUBIC * values * values)
    return 0.5 * (1.0 + tangent) + outer


def conv_backward(crops, weight, upstream):
    box_count = crops.shape[0]
    crop_side = crops.shape[1]
    channels = crops.shape[3]
    padded = jnp.pad(crops, ((0, 0), (1, 1), (1, 1), (0, 0)))
    windows = []
    for tap_index in range(9):
        tap_row = tap_index // 3
        tap_col = tap_index % 3
        windows.append(padded[:, tap_row:tap_row + crop_side, tap_col:tap_col + crop_side, :].reshape(-1, channels))
    pre_act = jnp.zeros((windows[0].shape[0], weight.shape[2]), jnp.float32)
    for tap_index in range(9):
        pre_act = pre_act + jnp.dot(windows[tap_index], weight[tap_index], preferred_element_type=jnp.float32)
    slope = (upstream.reshape(pre_act.shape).astype(jnp.float32) * gelu_slope(pre_act)).astype(jnp.bfloat16)
    weight_list = []
    for tap_index in range(9):
        weight_list.append(lax.dot_general(windows[tap_index], slope, (((0,), (0,)), ((), ())), preferred_element_type=jnp.float32))
    weight_terms = jnp.stack(weight_list)
    grad_pad = jnp.zeros((box_count, crop_side + 2, crop_side + 2, channels), jnp.float32)
    for tap_index in range(9):
        tap_row = tap_index // 3
        tap_col = tap_index % 3
        part_grad = lax.dot_general(slope, weight[tap_index], (((1,), (1,)), ((), ())), preferred_element_type=jnp.float32)
        grad_pad = grad_pad.at[:, tap_row:tap_row + crop_side, tap_col:tap_col + crop_side, :].add(part_grad.reshape(box_count, crop_side, crop_side, channels))
    crop_grad = grad_pad[:, 1:crop_side + 1, 1:crop_side + 1, :].astype(jnp.bfloat16)
    return weight_terms, crop_grad


def selector(live, slot_total):
    ranks = jnp.cumsum(live) - 1
    targets = lax.broadcasted_iota(jnp.int32, (slot_total, live.shape[0]), 0)
    chosen = (ranks[None, :] == targets) & (live[None, :] > 0)
    return chosen.astype(jnp.bfloat16)


def cut_crops(extended, top_rows, left_cols, crop_side):
    def single(top_row, left_col):
        return lax.dynamic_slice(extended, (top_row, left_col, top_row * 0), (crop_side, crop_side, extended.shape[2]))
    return jax.vmap(single)(top_rows, left_cols)


def add_crops(canvas, pieces, top_rows, left_cols, live):
    crop_side = pieces.shape[1]
    channels = canvas.shape[2]

    def place(slot_index, running):
        anchor = (top_rows[slot_index], left_cols[slot_index], top_rows[slot_index] * 0)
        current = lax.dynamic_slice(running, anchor, (crop_side, crop_side, channels))
        update = current + pieces[slot_index].astype(running.dtype) * live[slot_index]
        return lax.dynamic_update_slice(running, update, anchor)
    return lax.fori_loop(0, pieces.shape[0], place, canvas)


def reference(feature_map, weight, mask_grad, send_count, send_row, send_col):
    images = feature_map.shape[0]
    map_width = feature_map.shape[2]
    channels = feature_map.shape[3]
    tiles = send_count.shape[1]
    tile_height = feature_map.shape[1] // tiles
    boxes_head = mask_grad.shape[2]
    crop_side = mask_grad.shape[3]
    halo_rows = crop_side - 1
    slot_cap = send_row.shape[3]
    padded_map = jnp.concatenate([feature_map, jnp.zeros((images, halo_rows, map_width, channels), jnp.bfloat16)], 1)
    slot_iota = lax.broadcasted_iota(jnp.int32, (images, images, slot_cap), 2)

    def cutter(extended, top_rows, left_cols):
        return cut_crops(extended, top_rows, left_cols, crop_side)

    def column(carry, tile_id):
        spill, weight_total = carry
        extended = lax.dynamic_slice_in_dim(padded_map, tile_id * tile_height, tile_height + halo_rows, 1)
        top_rows = lax.dynamic_index_in_dim(send_row, tile_id, 1, keepdims=False).reshape(images, -1)
        left_cols = lax.dynamic_index_in_dim(send_col, tile_id, 1, keepdims=False).reshape(images, -1)
        counts = lax.dynamic_index_in_dim(send_count, tile_id, 1, keepdims=False)
        live = (slot_iota < counts[:, :, None]).astype(jnp.int32)
        crops = jax.vmap(cutter)(extended, top_rows, left_cols).reshape(images, images, slot_cap, -1)
        pickers = []
        head_boxes = []
        for head in range(images):
            picker = selector(live[:, head].reshape(-1), boxes_head)
            pickers.append(picker)
            flat = crops[:, head].reshape(images * slot_cap, -1)
            head_boxes.append(jnp.dot(picker, flat, preferred_element_type=jnp.float32).astype(jnp.bfloat16))
        all_boxes = jnp.concatenate(head_boxes, 0).reshape(images * boxes_head, crop_side, crop_side, channels)
        upstream = lax.dynamic_index_in_dim(mask_grad, tile_id, 1, keepdims=False).reshape(images * boxes_head, crop_side, crop_side, channels)
        weight_terms, crop_grad = conv_backward(all_boxes, weight, upstream)
        crop_flat = crop_grad.reshape(images, boxes_head, -1)
        slot_list = []
        for head in range(images):
            back = jnp.dot(pickers[head].T, crop_flat[head], preferred_element_type=jnp.float32).astype(jnp.bfloat16)
            slot_list.append(back.reshape(images, slot_cap, -1))
        slot_grads = jnp.stack(slot_list, 1).reshape(images, images * slot_cap, crop_side, crop_side, channels)
        canvas = jnp.zeros((images, tile_height + halo_rows, map_width, channels), jnp.float32)
        canvas = jax.vmap(add_crops)(canvas, slot_grads, top_rows, left_cols, live.reshape(images, -1).astype(jnp.float32))
        main = jnp.concatenate([canvas[:, :halo_rows] + spill, canvas[:, halo_rows:tile_height]], 1)
        return (canvas[:, tile_height:], weight_total + weight_terms), main

    start_spill = jnp.zeros((images, halo_rows, map_width, channels), jnp.float32)
    start_weight = jnp.zeros(weight.shape, jnp.float32)
    final, mains = lax.scan(column, (start_spill, start_weight), jnp.arange(tiles, dtype=jnp.int32))
    map_grad = jnp.transpose(mains, (1, 0, 2, 3, 4)).reshape(images, tiles * tile_height, map_width, channels)
    weight_grad = final[1] / (images * tiles * boxes_head)
    return map_grad, weight_grad
```

```python
import functools

import jax
import jax.numpy as jnp
from jax import lax
from jax.experimental import pallas as pl
from jax.experimental.pallas import tpu as pltpu
from jax.sharding import PartitionSpec as P

GELU_SCALE = 0.7978845608
GELU_CUBIC = 0.044715
LANES = 128
EDGE = 8
VMEM_BYTES = 40 * 1024 * 1024
VM = pl.BlockSpec(memory_space=pltpu.VMEM)
SM = pl.BlockSpec(memory_space=pltpu.SMEM)
LOCAL = pltpu.CompilerParams(vmem_limit_bytes=VMEM_BYTES)


def shifted(array, axis, by):
    length = lax.axis_size(axis)
    pairs = [(i, i + by) for i in range(length) if 0 <= i + by < length]
    return lax.ppermute(array, axis, pairs)


def rotated(array, axis, by):
    length = lax.axis_size(axis)
    return lax.ppermute(array, axis, [(i, (i + by) % length) for i in range(length)])


def gelu_slope(values):
    inner = GELU_SCALE * (values + GELU_CUBIC * values * values * values)
    tangent = jnp.tanh(inner)
    outer = (
        0.5
        * values
        * (1.0 - tangent * tangent)
        * GELU_SCALE
        * (1.0 + 3.0 * GELU_CUBIC * values * values)
    )
    return 0.5 * (1.0 + tangent) + outer


def cut_kernel(n, cap, side, wide, me_ref, count_ref, row_ref, col_ref, map_ref, below_ref, own_ref, send_ref, ext):
    height, width = map_ref.shape[0], map_ref.shape[1]
    ext[:height, EDGE : EDGE + width, :] = map_ref[...].astype(jnp.float32)
    ext[height:, EDGE : EDGE + width, :] = below_ref[...].astype(jnp.float32)
    me = me_ref[0]
    span = 2 * wide
    cell = lax.broadcasted_iota(jnp.int32, (wide, map_ref.shape[2]), 0)
    inside = (cell >= 1) & (cell <= side)
    for k in range(n):
        head = lax.rem(me + k, n)
        for r in range(cap):
            slot = head * cap + r
            top, place = row_ref[slot], col_ref[slot] + EDGE - 1
            base = pl.multiple_of(place // 8 * 8, 8)
            back = lax.rem(span - lax.rem(place, 8), span)
            flag = jnp.where(r < count_ref[head], 1.0, 0.0)
            for y in range(side):
                line = pltpu.roll(ext[top + y, pl.ds(base, span), :], back, 0)[:wide]
                line = jnp.where(inside, line, 0.0)
                if y == 0:
                    line = jnp.where(cell == wide - 1, flag, line)
                line = line.astype(jnp.bfloat16)
                if k == 0:
                    own_ref[r, y] = line
                else:
                    send_ref[k - 1, r, y] = line


def conv_kernel(n, cap, boxes, side, wide, me_ref, own_ref, got_ref, weight_ref, up_ref,
                back_own, back_send, terms_ref, slots, shift, x3, s3, sl, cg, picks):
    channels = weight_ref.shape[2]
    area, full = side * wide, (side + 2) * wide
    me = me_ref[0]
    slots[me] = own_ref[...]
    for k in range(1, n):
        slots[lax.rem(me + n - k, n)] = got_ref[k - 1]
    cell = lax.broadcasted_iota(jnp.int32, (1, wide, channels), 1)
    inside = (cell >= 1) & (cell <= side)
    rank = jnp.zeros((1, channels), jnp.float32)
    for i in range(n):
        for r in range(cap):
            flag = slots[i, r, 0][wide - 1 : wide, :].astype(jnp.float32)
            for b in range(boxes):
                picks[b, i * cap + r] = flag * jnp.where(rank == float(b), 1.0, 0.0)
            rank = rank + flag
    shift[...] = jnp.zeros_like(shift)
    for b in range(boxes):
        box = jnp.zeros((side, wide, channels), jnp.float32)
        for i in range(n):
            for r in range(cap):
                box = box + slots[i, r].astype(jnp.float32) * picks[b, i * cap + r][None]
        box = jnp.where(inside, box, 0.0).reshape(area, channels)
        shift[EDGE + wide : EDGE + wide + area, :] = box
        for t in range(3):
            x3[b, :, t * channels : (t + 1) * channels] = shift[
                EDGE - 1 + t : EDGE - 1 + t + full, :
            ].astype(jnp.bfloat16)
        pre = jnp.zeros((area, channels), jnp.float32)
        for a in range(3):
            pre = pre + jnp.dot(
                x3[b, wide * a : wide * a + area, :],
                weight_ref[3 * a : 3 * a + 3].reshape(3 * channels, channels),
                preferred_element_type=jnp.float32,
            )
        slope = (up_ref[b].reshape(area, channels).astype(jnp.float32) * gelu_slope(pre)).astype(jnp.bfloat16)
        sl[b] = slope
        shift[EDGE + wide : EDGE + wide + area, :] = slope.astype(jnp.float32)
        for t in range(3):
            s3[b, :, t * channels : (t + 1) * channels] = shift[
                EDGE + 1 - t : EDGE + 1 - t + full, :
            ].astype(jnp.bfloat16)
        grad = jnp.zeros((area, channels), jnp.float32)
        for a in range(3):
            for t in range(3):
                grad = grad + lax.dot_general(
                    s3[b, wide * (2 - a) : wide * (2 - a) + area, t * channels : (t + 1) * channels],
                    weight_ref[3 * a + t],
                    (((1,), (1,)), ((), ())),
                    preferred_element_type=jnp.float32,
                )
        grad = jnp.where(inside, grad.reshape(side, wide, channels), 0.0)
        cg[b] = grad.astype(jnp.bfloat16)
    for k in range(n):
        i = lax.rem(me + n - k, n)
        for r in range(cap):
            back = jnp.zeros((side, wide, channels), jnp.float32)
            for b in range(boxes):
                back = back + cg[b].astype(jnp.float32) * picks[b, i * cap + r][None]
            if k == 0:
                back_own[r] = back.astype(jnp.bfloat16)
            else:
                back_send[k - 1, r] = back.astype(jnp.bfloat16)
    for a in range(3):
        total = jnp.zeros((3 * channels, channels), jnp.float32)
        for b in range(boxes):
            total = total + lax.dot_general(
                x3[b, wide * a : wide * a + area, :], sl[b], (((0,), (0,)), ((), ())),
                preferred_element_type=jnp.float32,
            )
        depth = 3 * channels
        for h in range(channels // LANES):
            start = h * 3 * depth + a * depth
            terms_ref[start : start + depth, :] = total[:, h * LANES : (h + 1) * LANES]


def paste_kernel(n, cap, side, wide, me_ref, count_ref, row_ref, col_ref, own_ref, got_ref, main_ref, spill_ref, canvas):
    height, width = main_ref.shape[0], main_ref.shape[1]
    canvas[...] = jnp.zeros_like(canvas)
    me = me_ref[0]
    for k in range(n):
        head = lax.rem(me + k, n)
        for r in range(cap):

            @pl.when(r < count_ref[head])
            def _():
                top, place = row_ref[head * cap + r], col_ref[head * cap + r] + EDGE - 1
                base = pl.multiple_of(place // 8 * 8, 8)
                ahead = lax.rem(place, 8)
                for y in range(side):
                    line = (own_ref[r, y] if k == 0 else got_ref[k - 1, r, y]).astype(jnp.float32)
                    line = jnp.concatenate([line, jnp.zeros_like(line)], 0)
                    window = (top + y, pl.ds(base, 2 * wide), slice(None))
                    canvas[window] = canvas[window] + pltpu.roll(line, ahead, 0)

    main_ref[...] = canvas[:height, EDGE : EDGE + width, :]
    spill_ref[...] = canvas[height:, EDGE : EDGE + width, :].astype(spill_ref.dtype)


def bits_of(name, length):
    return [(name, 1 << i) for i in range(length.bit_length() - 1)]


def plan(tiles, heads, rows):
    tile_bits = bits_of("tile", tiles)
    order = tile_bits[:2] + bits_of("dp", heads) + tile_bits[2:]
    steps, size = [], rows
    for index, (name, bit) in enumerate(order):
        halves = size % 32 == 0
        size = size // 2 if halves else size
        narrow = halves and 0 < index < 3
        steps.append((name, bit, halves, size, narrow))
    return steps


def partner_of(name, bit):
    here = lax.axis_index(name)
    side = lax.rem(here // bit, 2)
    return side, {name: here + bit - 2 * bit * side}


def greet(steps):
    barrier = pltpu.get_barrier_semaphore()
    for name, bit, *_ in steps:
        pl.semaphore_signal(
            barrier, inc=1, device_id=partner_of(name, bit)[1], device_id_type=pl.DeviceIdType.MESH
        )
    pl.semaphore_wait(barrier, len(steps))


def scatter_kernel(steps, terms_ref, out_ref, total, send_sem, recv_sem, *bufs):
    count = len(steps)
    landing, staged = bufs[:count], bufs[count:]
    greet(steps)
    total[...] = terms_ref[...]
    base = 0
    stage_at = 0
    for index, (name, bit, halves, size, narrow) in enumerate(steps):
        side, other = partner_of(name, bit)
        if halves:
            keep = pl.multiple_of(base + side * size, 16)
            give = pl.multiple_of(base + (1 - side) * size, 16)
        else:
            keep, give = base, base
        if narrow:
            staged[stage_at][...] = total[pl.ds(give, size), :].astype(jnp.bfloat16)
            source = staged[stage_at]
            stage_at += 1
        else:
            source = total.at[pl.ds(give, size), :]
        copy = pltpu.make_async_remote_copy(
            src_ref=source, dst_ref=landing[index], send_sem=send_sem.at[index], recv_sem=recv_sem.at[index],
            device_id=other, device_id_type=pl.DeviceIdType.MESH,
        )
        copy.start()
        copy.wait()
        total[pl.ds(keep, size), :] = total[pl.ds(keep, size), :] + landing[index][...].astype(jnp.float32)
        base = keep
    out_ref[...] = total[pl.ds(base, steps[-1][3]), :].astype(out_ref.dtype)


def gather_kernel(steps, part_ref, out_ref, whole, send_sem, recv_sem):
    halving = [s for s in steps if s[2]]
    greet(halving)
    bases = [0]
    for name, bit, _, size, _ in halving:
        bases.append(pl.multiple_of(bases[-1] + partner_of(name, bit)[0] * size, 16))
    whole[pl.ds(bases[-1], halving[-1][3]), :] = part_ref[...]
    for index in reversed(range(len(halving))):
        name, bit, _, size, _ = halving[index]
        mine = whole.at[pl.ds(bases[index + 1], size), :]
        copy = pltpu.make_async_remote_copy(
            src_ref=mine, dst_ref=mine, send_sem=send_sem.at[index], recv_sem=recv_sem.at[index],
            device_id=partner_of(name, bit)[1], device_id_type=pl.DeviceIdType.MESH,
        )
        copy.start()
        copy.wait()
    out_ref[...] = whole[...]


def reduce_scatter(terms, tiles, heads):
    rows = terms.shape[0]
    steps = plan(tiles, heads, rows)
    count = len(steps)
    landing = [pltpu.VMEM((s[3], LANES), jnp.bfloat16 if s[4] else jnp.float32) for s in steps]
    staged = [pltpu.VMEM((s[3], LANES), jnp.bfloat16) for s in steps if s[4]]
    return pl.pallas_call(
        functools.partial(scatter_kernel, steps),
        out_shape=jax.ShapeDtypeStruct((steps[-1][3], LANES), jnp.bfloat16),
        in_specs=[VM],
        out_specs=VM,
        scratch_shapes=[
            pltpu.VMEM(terms.shape, jnp.float32),
            pltpu.SemaphoreType.DMA((count,)),
            pltpu.SemaphoreType.DMA((count,)),
            *landing,
            *staged,
        ],
        compiler_params=pltpu.CompilerParams(
            collective_id=0, has_side_effects=True, vmem_limit_bytes=VMEM_BYTES
        ),
        cost_estimate=pl.CostEstimate(flops=10**6, bytes_accessed=50 * 10**6, transcendentals=0),
        name="term_scatter",
    )(terms)


def gather(part, tiles, heads, rows):
    steps = plan(tiles, heads, rows)
    count = len(steps)
    return pl.pallas_call(
        functools.partial(gather_kernel, steps),
        out_shape=jax.ShapeDtypeStruct((rows, LANES), jnp.bfloat16),
        in_specs=[VM],
        out_specs=VM,
        scratch_shapes=[
            pltpu.VMEM((rows, LANES), jnp.bfloat16),
            pltpu.SemaphoreType.DMA((count,)),
            pltpu.SemaphoreType.DMA((count,)),
        ],
        compiler_params=pltpu.CompilerParams(
            collective_id=1, has_side_effects=True, vmem_limit_bytes=VMEM_BYTES
        ),
        cost_estimate=pl.CostEstimate(flops=10**6, bytes_accessed=50 * 10**6, transcendentals=0),
        name="term_gather",
    )(part)


def on_device(feature_map, weight, mask_grad, send_count, send_row, send_col):
    tile_map = feature_map[0]
    height, width, channels = tile_map.shape
    boxes, side = mask_grad.shape[2], mask_grad.shape[3]
    wide = -(-(side + 2) // 16) * 16
    halo = side - 1
    n, cap = send_row.shape[2], send_row.shape[3]
    tiles, heads = lax.axis_size("tile"), lax.axis_size("dp")
    others = max(n - 1, 1)
    below = shifted(tile_map[:halo], "tile", -1)
    me = lax.axis_index("dp").reshape(1)
    counts = send_count.reshape(-1)
    tops, lefts = send_row.reshape(-1), send_col.reshape(-1)
    room = EDGE + width + 2 * EDGE
    own_shape = jax.ShapeDtypeStruct((cap, side, wide, channels), jnp.bfloat16)
    send_shape = jax.ShapeDtypeStruct((others, cap, side, wide, channels), jnp.bfloat16)
    own, send = pl.pallas_call(
        functools.partial(cut_kernel, n, cap, side, wide),
        out_shape=(own_shape, send_shape),
        in_specs=[SM, SM, SM, SM, VM, VM],
        out_specs=(VM, VM),
        scratch_shapes=[pltpu.VMEM((height + halo, room, channels), jnp.float32)],
        compiler_params=LOCAL,
        name="cut",
    )(me, counts, tops, lefts, tile_map, below)

    def swapped(array, sign):
        parts = [rotated(array[k - 1], "dp", sign * k) for k in range(1, n)]
        return jnp.stack(parts) if len(parts) > 1 else parts[0][None]

    got = swapped(send, 1)
    upstream = jnp.pad(mask_grad[0, 0], ((0, 0), (0, 0), (1, wide - side - 1), (0, 0)))
    full = (side + 2) * wide
    rows = 9 * channels * (channels // LANES)
    back_own, back_send, terms = pl.pallas_call(
        functools.partial(conv_kernel, n, cap, boxes, side, wide),
        out_shape=(own_shape, send_shape, jax.ShapeDtypeStruct((rows, LANES), jnp.float32)),
        in_specs=[SM, VM, VM, VM, VM],
        out_specs=(VM, VM, VM),
        scratch_shapes=[
            pltpu.VMEM((n, cap, side, wide, channels), jnp.bfloat16),
            pltpu.VMEM((full + 2 * EDGE, channels), jnp.float32),
            pltpu.VMEM((boxes, full, 3 * channels), jnp.bfloat16),
            pltpu.VMEM((boxes, full, 3 * channels), jnp.bfloat16),
            pltpu.VMEM((boxes, side * wide, channels), jnp.bfloat16),
            pltpu.VMEM((boxes, side, wide, channels), jnp.bfloat16),
            pltpu.VMEM((boxes, n * cap, 1, channels), jnp.float32),
        ],
        compiler_params=LOCAL,
        name="conv",
    )(me, own, got, weight, upstream)
    back_got = swapped(back_send, -1)
    part = reduce_scatter(terms, tiles, heads)
    main, spill = pl.pallas_call(
        functools.partial(paste_kernel, n, cap, side, wide),
        out_shape=(
            jax.ShapeDtypeStruct((height, width, channels), jnp.float32),
            jax.ShapeDtypeStruct((halo, width, channels), jnp.bfloat16),
        ),
        in_specs=[SM, SM, SM, SM, VM, VM],
        out_specs=(VM, VM),
        scratch_shapes=[pltpu.VMEM((height + halo, room, channels), jnp.float32)],
        compiler_params=LOCAL,
        name="paste",
    )(me, counts, tops, lefts, back_own, back_got)
    arriving = shifted(spill, "tile", 1)
    whole = gather(part, tiles, heads, rows)
    map_grad = main.at[:halo].add(arriving.astype(jnp.float32))
    box_total = boxes * tiles * heads
    halves = whole.reshape(channels // LANES, 9 * channels, LANES)
    summed = jnp.concatenate([halves[h] for h in range(channels // LANES)], -1)
    weight_grad = summed.reshape(9, channels, channels).astype(jnp.float32) / box_total
    return (map_grad[None], weight_grad)


def solution(mesh):
    in_specs = (
        P("dp", "tile", None, None),
        P(),
        P("dp", "tile", None, None, None, None),
        P("dp", "tile", None),
        P("dp", "tile", None, None),
        P("dp", "tile", None, None),
    )
    out_specs = (P("dp", "tile", None, None), P())
    return jax.shard_map(
        on_device, mesh=mesh, in_specs=in_specs, out_specs=out_specs, check_vma=False
    )
```

```python
import functools

import jax
import jax.numpy as jnp
from jax import lax
from jax.experimental import pallas as pl
from jax.experimental.pallas import tpu as pltpu
from jax.sharding import PartitionSpec as P

GELU_SCALE = 0.7978845608
GELU_CUBIC = 0.044715
LANES = 128
EDGE = 8
VMEM_BYTES = 40 * 1024 * 1024
VM = pl.BlockSpec(memory_space=pltpu.VMEM)
SM = pl.BlockSpec(memory_space=pltpu.SMEM)
LOCAL = pltpu.CompilerParams(vmem_limit_bytes=VMEM_BYTES)


def shifted(array, axis, by):
    length = lax.axis_size(axis)
    pairs = [(i, i + by) for i in range(length) if 0 <= i + by < length]
    return lax.ppermute(array, axis, pairs)


def rotated(array, axis, by):
    length = lax.axis_size(axis)
    return lax.ppermute(array, axis, [(i, (i + by) % length) for i in range(length)])


def gelu_slope(values):
    inner = GELU_SCALE * (values + GELU_CUBIC * values * values * values)
    tangent = jnp.tanh(inner)
    outer = (
        0.5
        * values
        * (1.0 - tangent * tangent)
        * GELU_SCALE
        * (1.0 + 3.0 * GELU_CUBIC * values * values)
    )
    return 0.5 * (1.0 + tangent) + outer


def cut_kernel(n, cap, side, wide, me_ref, count_ref, row_ref, col_ref, map_ref, below_ref, own_ref, send_ref, ext):
    height, width = map_ref.shape[0], map_ref.shape[1]
    ext[:height, EDGE : EDGE + width, :] = map_ref[...].astype(jnp.float32)
    ext[height:, EDGE : EDGE + width, :] = below_ref[...].astype(jnp.float32)
    me = me_ref[0]
    span = 2 * wide
    cell = lax.broadcasted_iota(jnp.int32, (wide, map_ref.shape[2]), 0)
    inside = (cell >= 1) & (cell <= side)
    for k in range(n):
        head = lax.rem(me + k, n)
        for r in range(cap):
            slot = head * cap + r
            top, place = row_ref[slot], col_ref[slot] + EDGE - 1
            base = pl.multiple_of(place // 8 * 8, 8)
            back = lax.rem(span - lax.rem(place, 8), span)
            flag = jnp.where(r < count_ref[head], 1.0, 0.0)
            for y in range(side):
                line = pltpu.roll(ext[top + y, pl.ds(base, span), :], back, 0)[:wide]
                line = jnp.where(inside, line, 0.0)
                if y == 0:
                    line = jnp.where(cell == wide - 1, flag, line)
                line = line.astype(jnp.bfloat16)
                if k == 0:
                    own_ref[r, y] = line
                else:
                    send_ref[k - 1, r, y] = line


def conv_kernel(n, cap, boxes, side, wide, me_ref, own_ref, got_ref, weight_ref, up_ref,
                back_own, back_send, terms_ref, slots, shift, x3, s3, sl, cg, picks):
    channels = weight_ref.shape[2]
    area, full = side * wide, (side + 2) * wide
    me = me_ref[0]
    slots[me] = own_ref[...]
    for k in range(1, n):
        slots[lax.rem(me + n - k, n)] = got_ref[k - 1]
    cell = lax.broadcasted_iota(jnp.int32, (1, wide, channels), 1)
    inside = (cell >= 1) & (cell <= side)
    rank = jnp.zeros((1, channels), jnp.float32)
    for i in range(n):
        for r in range(cap):
            flag = slots[i, r, 0][wide - 1 : wide, :].astype(jnp.float32)
            for b in range(boxes):
                picks[b, i * cap + r] = flag * jnp.where(rank == float(b), 1.0, 0.0)
            rank = rank + flag
    shift[...] = jnp.zeros_like(shift)
    for b in range(boxes):
        box = jnp.zeros((side, wide, channels), jnp.float32)
        for i in range(n):
            for r in range(cap):
                box = box + slots[i, r].astype(jnp.float32) * picks[b, i * cap + r][None]
        box = jnp.where(inside, box, 0.0).reshape(area, channels)
        shift[EDGE + wide : EDGE + wide + area, :] = box
        for t in range(3):
            x3[b, :, t * channels : (t + 1) * channels] = shift[
                EDGE - 1 + t : EDGE - 1 + t + full, :
            ].astype(jnp.bfloat16)
        pre = jnp.zeros((area, channels), jnp.float32)
        for a in range(3):
            pre = pre + jnp.dot(
                x3[b, wide * a : wide * a + area, :],
                weight_ref[3 * a : 3 * a + 3].reshape(3 * channels, channels),
                preferred_element_type=jnp.float32,
            )
        slope = (up_ref[b].reshape(area, channels).astype(jnp.float32) * gelu_slope(pre)).astype(jnp.bfloat16)
        sl[b] = slope
        shift[EDGE + wide : EDGE + wide + area, :] = slope.astype(jnp.float32)
        for t in range(3):
            s3[b, :, t * channels : (t + 1) * channels] = shift[
                EDGE + 1 - t : EDGE + 1 - t + full, :
            ].astype(jnp.bfloat16)
        grad = jnp.zeros((area, channels), jnp.float32)
        for a in range(3):
            for t in range(3):
                grad = grad + lax.dot_general(
                    s3[b, wide * (2 - a) : wide * (2 - a) + area, t * channels : (t + 1) * channels],
                    weight_ref[3 * a + t],
                    (((1,), (1,)), ((), ())),
                    preferred_element_type=jnp.float32,
                )
        grad = jnp.where(inside, grad.reshape(side, wide, channels), 0.0)
        cg[b] = grad.astype(jnp.bfloat16)
    for k in range(n):
        i = lax.rem(me + n - k, n)
        for r in range(cap):
            back = jnp.zeros((side, wide, channels), jnp.float32)
            for b in range(boxes):
                back = back + cg[b].astype(jnp.float32) * picks[b, i * cap + r][None]
            if k == 0:
                back_own[r] = back.astype(jnp.bfloat16)
            else:
                back_send[k - 1, r] = back.astype(jnp.bfloat16)
    for a in range(3):
        total = jnp.zeros((3 * channels, channels), jnp.float32)
        for b in range(boxes):
            total = total + lax.dot_general(
                x3[b, wide * a : wide * a + area, :], sl[b], (((0,), (0,)), ((), ())),
                preferred_element_type=jnp.float32,
            )
        depth = 3 * channels
        for h in range(channels // LANES):
            start = h * 3 * depth + a * depth
            terms_ref[start : start + depth, :] = total[:, h * LANES : (h + 1) * LANES]


def paste_kernel(n, cap, side, wide, me_ref, count_ref, row_ref, col_ref, own_ref, got_ref, main_ref, spill_ref, canvas):
    height, width = main_ref.shape[0], main_ref.shape[1]
    canvas[...] = jnp.zeros_like(canvas)
    me = me_ref[0]
    for k in range(n):
        head = lax.rem(me + k, n)
        for r in range(cap):

            @pl.when(r < count_ref[head])
            def _():
                top, place = row_ref[head * cap + r], col_ref[head * cap + r] + EDGE - 1
                base = pl.multiple_of(place // 8 * 8, 8)
                ahead = lax.rem(place, 8)
                for y in range(side):
                    line = (own_ref[r, y] if k == 0 else got_ref[k - 1, r, y]).astype(jnp.float32)
                    line = jnp.concatenate([line, jnp.zeros_like(line)], 0)
                    window = (top + y, pl.ds(base, 2 * wide), slice(None))
                    canvas[window] = canvas[window] + pltpu.roll(line, ahead, 0)

    main_ref[...] = canvas[:height, EDGE : EDGE + width, :]
    spill_ref[...] = canvas[height:, EDGE : EDGE + width, :].astype(spill_ref.dtype)


def bits_of(name, length):
    return [(name, 1 << i) for i in range(length.bit_length() - 1)]


def part_steps(order, rows):
    steps, size = [], rows
    for name, stride, radix in order:
        if size % (16 * radix) == 0:
            size = size // radix
            steps.append((name, stride, radix, True, size))
        else:
            digits = radix.bit_length() - 1
            steps.extend((name, stride << i, 2, False, size) for i in range(digits))
    return steps


def plan(tiles, heads, rows):
    tile_bits = [(name, bit, 2) for name, bit in bits_of("tile", tiles)]
    head_bits = [(name, bit, 2) for name, bit in bits_of("dp", heads)]
    first, second, far = tile_bits[:1], tile_bits[1:2], tile_bits[2:]
    if len(far) % 2 == 0:
        far = [(name, bit, 4) for name, bit, _ in far[::2]]
    unit = 16 * 32
    top = -(-(rows // unit) // 2) * unit
    return [
        (0, part_steps(first + second + head_bits + far, top)),
        (top, part_steps(first + head_bits + second + far, rows - top)),
    ]


def peer(name, stride, radix, hop):
    here = lax.axis_index(name)
    digit = lax.rem(here // stride, radix)
    other = lax.rem(digit + hop, radix)
    return digit, other, {name: here + (other - digit) * stride}


def greet(parts):
    kinds = sorted({step[:3] for _, steps in parts for step in steps})
    barrier = pltpu.get_barrier_semaphore()
    count = 0
    for name, stride, radix in kinds:
        for hop in range(1, radix):
            pl.semaphore_signal(
                barrier, inc=1, device_id=peer(name, stride, radix, hop)[2],
                device_id_type=pl.DeviceIdType.MESH,
            )
            count += 1
    pl.semaphore_wait(barrier, count)


def walk(part_at, begin, steps, landings, stages, terms_ref, total, whole, send_sem, recv_sem):
    base, wire = begin, 0
    bases = [begin]

    def copy_to(source, target, device):
        nonlocal wire
        copy = pltpu.make_async_remote_copy(
            src_ref=source, dst_ref=target, send_sem=send_sem.at[part_at, wire], recv_sem=recv_sem.at[part_at, wire],
            device_id=device, device_id_type=pl.DeviceIdType.MESH,
        )
        wire += 1
        copy.start()
        return copy

    for index, (name, stride, radix, halves, size) in enumerate(steps):
        held = terms_ref if index == 0 else total
        copies = []
        for hop in range(1, radix):
            digit, other, device = peer(name, stride, radix, hop)
            give = pl.multiple_of(base + other * size, 16) if halves else base
            landing = landings[index].at[hop - 1]
            if halves and index > 0:
                stage = stages[index].at[hop - 1]
                stage[...] = held[pl.ds(give, size), :].astype(jnp.bfloat16)
                copies.append(copy_to(stage, landing, device))
            else:
                copies.append(copy_to(held.at[pl.ds(give, size), :], landing, device))
        yield
        keep = pl.multiple_of(base + digit * size, 16) if halves else base
        for copy in copies:
            copy.wait()
        value = held[pl.ds(keep, size), :]
        for hop in range(1, radix):
            value = value + landings[index][hop - 1].astype(jnp.float32)
        if index == len(steps) - 1:
            whole[pl.ds(keep, size), :] = value.astype(jnp.bfloat16)
        else:
            total[pl.ds(keep, size), :] = value
        if halves:
            bases.append(keep)
        base = keep
    halving = [step for step in steps if step[3]]
    for index in reversed(range(len(halving))):
        name, stride, radix, _, size = halving[index]
        mine = whole.at[pl.ds(bases[index + 1], size), :]
        copies = [
            copy_to(mine, mine, peer(name, stride, radix, hop)[2]) for hop in range(1, radix)
        ]
        yield
        for copy in copies:
            copy.wait()


def reduce_kernel(parts, layout, terms_ref, out_ref, total, whole, send_sem, recv_sem, *bufs):
    greet(parts)
    walks = []
    for at, (begin, steps) in enumerate(parts):
        landings, stages = [[bufs[i] if i is not None else None for i in row] for row in layout[at]]
        walks.append(
            walk(at, begin, steps, landings, stages, terms_ref, total, whole, send_sem, recv_sem)
        )
    while walks:
        walks = [w for w in walks if next(w, 0) is None]
    out_ref[...] = whole[...]


def reduced(terms, tiles, heads):
    rows = terms.shape[0]
    parts = plan(tiles, heads, rows)
    bufs, layout, wires = [], [], 0
    for _, steps in parts:
        landings, stages = [], []
        for index, (_, _, radix, halves, size) in enumerate(steps):
            narrow = halves and index > 0
            shape = (radix - 1, size, LANES)
            landings.append(len(bufs))
            bufs.append(pltpu.VMEM(shape, jnp.bfloat16 if narrow else jnp.float32))
            stages.append(len(bufs) if narrow else None)
            if narrow:
                bufs.append(pltpu.VMEM(shape, jnp.bfloat16))
        layout.append((landings, stages))
        wires = max(wires, sum(s[2] - 1 for s in steps) + sum(s[2] - 1 for s in steps if s[3]))
    return pl.pallas_call(
        functools.partial(reduce_kernel, parts, layout),
        out_shape=jax.ShapeDtypeStruct((rows, LANES), jnp.bfloat16),
        in_specs=[VM],
        out_specs=VM,
        scratch_shapes=[
            pltpu.VMEM(terms.shape, jnp.float32),
            pltpu.VMEM(terms.shape, jnp.bfloat16),
            pltpu.SemaphoreType.DMA((len(parts), wires)),
            pltpu.SemaphoreType.DMA((len(parts), wires)),
            *bufs,
        ],
        compiler_params=pltpu.CompilerParams(
            collective_id=0, has_side_effects=True, vmem_limit_bytes=VMEM_BYTES
        ),
        cost_estimate=pl.CostEstimate(flops=10**6, bytes_accessed=100 * 10**6, transcendentals=0),
        name="term_sum",
    )(terms)


def on_device(feature_map, weight, mask_grad, send_count, send_row, send_col):
    tile_map = feature_map[0]
    height, width, channels = tile_map.shape
    boxes, side = mask_grad.shape[2], mask_grad.shape[3]
    wide = -(-(side + 2) // 16) * 16
    halo = side - 1
    n, cap = send_row.shape[2], send_row.shape[3]
    tiles, heads = lax.axis_size("tile"), lax.axis_size("dp")
    others = max(n - 1, 1)
    below = shifted(tile_map[:halo], "tile", -1)
    me = lax.axis_index("dp").reshape(1)
    counts = send_count.reshape(-1)
    tops, lefts = send_row.reshape(-1), send_col.reshape(-1)
    room = EDGE + width + 2 * EDGE
    own_shape = jax.ShapeDtypeStruct((cap, side, wide, channels), jnp.bfloat16)
    send_shape = jax.ShapeDtypeStruct((others, cap, side, wide, channels), jnp.bfloat16)
    own, send = pl.pallas_call(
        functools.partial(cut_kernel, n, cap, side, wide),
        out_shape=(own_shape, send_shape),
        in_specs=[SM, SM, SM, SM, VM, VM],
        out_specs=(VM, VM),
        scratch_shapes=[pltpu.VMEM((height + halo, room, channels), jnp.float32)],
        compiler_params=LOCAL,
        name="cut",
    )(me, counts, tops, lefts, tile_map, below)

    def swapped(array, sign):
        parts = [rotated(array[k - 1], "dp", sign * k) for k in range(1, n)]
        return jnp.stack(parts) if len(parts) > 1 else parts[0][None]

    got = swapped(send, 1)
    upstream = jnp.pad(mask_grad[0, 0], ((0, 0), (0, 0), (1, wide - side - 1), (0, 0)))
    full = (side + 2) * wide
    rows = 9 * channels * (channels // LANES)
    back_own, back_send, terms = pl.pallas_call(
        functools.partial(conv_kernel, n, cap, boxes, side, wide),
        out_shape=(own_shape, send_shape, jax.ShapeDtypeStruct((rows, LANES), jnp.float32)),
        in_specs=[SM, VM, VM, VM, VM],
        out_specs=(VM, VM, VM),
        scratch_shapes=[
            pltpu.VMEM((n, cap, side, wide, channels), jnp.bfloat16),
            pltpu.VMEM((full + 2 * EDGE, channels), jnp.float32),
            pltpu.VMEM((boxes, full, 3 * channels), jnp.bfloat16),
            pltpu.VMEM((boxes, full, 3 * channels), jnp.bfloat16),
            pltpu.VMEM((boxes, side * wide, channels), jnp.bfloat16),
            pltpu.VMEM((boxes, side, wide, channels), jnp.bfloat16),
            pltpu.VMEM((boxes, n * cap, 1, channels), jnp.float32),
        ],
        compiler_params=LOCAL,
        name="conv",
    )(me, own, got, weight, upstream)
    back_got = swapped(back_send, -1)
    whole = reduced(terms, tiles, heads)
    main, spill = pl.pallas_call(
        functools.partial(paste_kernel, n, cap, side, wide),
        out_shape=(
            jax.ShapeDtypeStruct((height, width, channels), jnp.float32),
            jax.ShapeDtypeStruct((halo, width, channels), jnp.bfloat16),
        ),
        in_specs=[SM, SM, SM, SM, VM, VM],
        out_specs=(VM, VM),
        scratch_shapes=[pltpu.VMEM((height + halo, room, channels), jnp.float32)],
        compiler_params=LOCAL,
        name="paste",
    )(me, counts, tops, lefts, back_own, back_got)
    arriving = shifted(spill, "tile", 1)
    map_grad = main.at[:halo].add(arriving.astype(jnp.float32))
    box_total = boxes * tiles * heads
    halves = whole.reshape(channels // LANES, 9 * channels, LANES)
    summed = jnp.concatenate([halves[h] for h in range(channels // LANES)], -1)
    weight_grad = summed.reshape(9, channels, channels).astype(jnp.float32) / box_total
    return (map_grad[None], weight_grad)


def solution(mesh):
    in_specs = (
        P("dp", "tile", None, None),
        P(),
        P("dp", "tile", None, None, None, None),
        P("dp", "tile", None),
        P("dp", "tile", None, None),
        P("dp", "tile", None, None),
    )
    out_specs = (P("dp", "tile", None, None), P())
    return jax.shard_map(
        on_device, mesh=mesh, in_specs=in_specs, out_specs=out_specs, check_vma=False
    )
```

```python
import functools

import jax
import jax.numpy as jnp
from jax import lax
from jax.experimental import pallas as pl
from jax.experimental.pallas import tpu as pltpu
from jax.sharding import PartitionSpec as P

GELU_SCALE = 0.7978845608
GELU_CUBIC = 0.044715
LANES = 128
EDGE = 8
VMEM_BYTES = 40 * 1024 * 1024
VM = pl.BlockSpec(memory_space=pltpu.VMEM)
SM = pl.BlockSpec(memory_space=pltpu.SMEM)
LOCAL = pltpu.CompilerParams(vmem_limit_bytes=VMEM_BYTES)


def shifted(array, axis, by):
    length = lax.axis_size(axis)
    pairs = [(i, i + by) for i in range(length) if 0 <= i + by < length]
    return lax.ppermute(array, axis, pairs)


def rotated(array, axis, by):
    length = lax.axis_size(axis)
    return lax.ppermute(array, axis, [(i, (i + by) % length) for i in range(length)])


def gelu_slope(values):
    inner = GELU_SCALE * (values + GELU_CUBIC * values * values * values)
    tangent = jnp.tanh(inner)
    outer = (
        0.5
        * values
        * (1.0 - tangent * tangent)
        * GELU_SCALE
        * (1.0 + 3.0 * GELU_CUBIC * values * values)
    )
    return 0.5 * (1.0 + tangent) + outer


def cut_kernel(n, cap, side, wide, me_ref, slots_ref, map_ref, below_ref, own_ref, send_ref, ext):
    height, width = map_ref.shape[0], map_ref.shape[1]
    ext[:height, EDGE : EDGE + width, :] = map_ref[...].astype(jnp.float32)
    ext[height:, EDGE : EDGE + width, :] = below_ref[...].astype(jnp.float32)
    me = me_ref[0]
    span = 2 * wide
    cell = lax.broadcasted_iota(jnp.int32, (wide, map_ref.shape[2]), 0)
    inside = (cell >= 1) & (cell <= side)
    for k in range(n):
        head = lax.rem(me + k, n)
        for r in range(cap):
            top, place = slots_ref[n + head * cap + r], slots_ref[n + (n + head) * cap + r] + EDGE - 1
            base = pl.multiple_of(place // 8 * 8, 8)
            back = lax.rem(span - lax.rem(place, 8), span)
            flag = jnp.where(r < slots_ref[head], 1.0, 0.0)
            for y in range(side):
                line = pltpu.roll(ext[top + y, pl.ds(base, span), :], back, 0)[:wide]
                line = jnp.where(inside, line, 0.0)
                if y == 0:
                    line = jnp.where(cell == wide - 1, flag, line)
                line = line.astype(jnp.bfloat16)
                if k == 0:
                    own_ref[r, y] = line
                else:
                    send_ref[k - 1, r, y] = line


def conv_kernel(n, cap, boxes, side, wide, me_ref, own_ref, got_ref, weight_ref, up_ref,
                back_own, back_send, x3, sl, slots, shift, s3, cg, picks):
    channels = weight_ref.shape[2]
    area, full = side * wide, (side + 2) * wide
    me = me_ref[0]
    slots[me] = own_ref[...]
    for k in range(1, n):
        slots[lax.rem(me + n - k, n)] = got_ref[k - 1]
    cell = lax.broadcasted_iota(jnp.int32, (1, wide, channels), 1)
    inside = (cell >= 1) & (cell <= side)
    rank = jnp.zeros((1, channels), jnp.float32)
    for i in range(n):
        for r in range(cap):
            flag = slots[i, r, 0][wide - 1 : wide, :].astype(jnp.float32)
            for b in range(boxes):
                picks[b, i * cap + r] = flag * jnp.where(rank == float(b), 1.0, 0.0)
            rank = rank + flag
    shift[...] = jnp.zeros_like(shift)
    for b in range(boxes):
        box = jnp.zeros((side, wide, channels), jnp.float32)
        for i in range(n):
            for r in range(cap):
                box = box + slots[i, r].astype(jnp.float32) * picks[b, i * cap + r][None]
        box = jnp.where(inside, box, 0.0).reshape(area, channels)
        shift[EDGE + wide : EDGE + wide + area, :] = box
        for t in range(3):
            x3[b, :, t * channels : (t + 1) * channels] = shift[
                EDGE - 1 + t : EDGE - 1 + t + full, :
            ].astype(jnp.bfloat16)
        pre = jnp.zeros((area, channels), jnp.float32)
        for a in range(3):
            pre = pre + jnp.dot(
                x3[b, wide * a : wide * a + area, :],
                weight_ref[3 * a : 3 * a + 3].reshape(3 * channels, channels),
                preferred_element_type=jnp.float32,
            )
        slope = (up_ref[b].reshape(area, channels).astype(jnp.float32) * gelu_slope(pre)).astype(jnp.bfloat16)
        sl[b] = slope
        shift[EDGE + wide : EDGE + wide + area, :] = slope.astype(jnp.float32)
        for t in range(3):
            s3[b, :, t * channels : (t + 1) * channels] = shift[
                EDGE + 1 - t : EDGE + 1 - t + full, :
            ].astype(jnp.bfloat16)
        grad = jnp.zeros((area, channels), jnp.float32)
        for a in range(3):
            for t in range(3):
                grad = grad + lax.dot_general(
                    s3[b, wide * (2 - a) : wide * (2 - a) + area, t * channels : (t + 1) * channels],
                    weight_ref[3 * a + t],
                    (((1,), (1,)), ((), ())),
                    preferred_element_type=jnp.float32,
                )
        grad = jnp.where(inside, grad.reshape(side, wide, channels), 0.0)
        cg[b] = grad.astype(jnp.bfloat16)
    for k in range(n):
        i = lax.rem(me + n - k, n)
        for r in range(cap):
            back = jnp.zeros((side, wide, channels), jnp.float32)
            for b in range(boxes):
                back = back + cg[b].astype(jnp.float32) * picks[b, i * cap + r][None]
            if k == 0:
                back_own[r] = back.astype(jnp.bfloat16)
            else:
                back_send[k - 1, r] = back.astype(jnp.bfloat16)


def terms_kernel(boxes, side, wide, x3, sl, terms_ref):
    channels, area = sl.shape[2], side * wide
    for a in range(3):
        total = jnp.zeros((3 * channels, channels), jnp.float32)
        for b in range(boxes):
            total = total + lax.dot_general(
                x3[b, wide * a : wide * a + area, :], sl[b], (((0,), (0,)), ((), ())),
                preferred_element_type=jnp.float32,
            )
        depth = 3 * channels
        for h in range(channels // LANES):
            start = h * 3 * depth + a * depth
            terms_ref[start : start + depth, :] = total[:, h * LANES : (h + 1) * LANES]


def paste_kernel(n, cap, side, wide, me_ref, slots_ref, own_ref, got_ref, main_ref, spill_ref, canvas):
    height, width = main_ref.shape[0], main_ref.shape[1]
    canvas[...] = jnp.zeros_like(canvas)
    me = me_ref[0]
    for k in range(n):
        head = lax.rem(me + k, n)
        for r in range(cap):

            @pl.when(r < slots_ref[head])
            def _():
                top, place = slots_ref[n + head * cap + r], slots_ref[n + (n + head) * cap + r] + EDGE - 1
                base = pl.multiple_of(place // 8 * 8, 8)
                ahead = lax.rem(place, 8)
                for y in range(side):
                    line = (own_ref[r, y] if k == 0 else got_ref[k - 1, r, y]).astype(jnp.float32)
                    line = jnp.concatenate([line, jnp.zeros_like(line)], 0)
                    window = (top + y, pl.ds(base, 2 * wide), slice(None))
                    canvas[window] = canvas[window] + pltpu.roll(line, ahead, 0)

    main_ref[...] = canvas[:height, EDGE : EDGE + width, :]
    spill_ref[...] = canvas[height:, EDGE : EDGE + width, :].astype(spill_ref.dtype)


def bits_of(name, length):
    return [(name, 1 << i) for i in range(length.bit_length() - 1)]


def part_steps(order, rows):
    steps, size = [], rows
    for name, stride, radix in order:
        if size % (16 * radix) == 0:
            size = size // radix
            steps.append((name, stride, radix, True, size))
        else:
            digits = radix.bit_length() - 1
            steps.extend((name, stride << i, 2, False, size) for i in range(digits))
    return steps


def plan(tiles, heads, rows):
    tile_bits = [(name, bit, 2) for name, bit in bits_of("tile", tiles)]
    head_bits = [(name, bit, 2) for name, bit in bits_of("dp", heads)]
    first, second, far = tile_bits[:1], tile_bits[1:2], tile_bits[2:]
    if len(far) % 2 == 0:
        far = [(name, bit, 4) for name, bit, _ in far[::2]]
    unit = 16 * 32
    parts, begin, pieces = [], 0, 4
    for at in range(pieces):
        size = ((rows // unit) // pieces + (at < (rows // unit) % pieces)) * unit
        near = second + head_bits if at % 2 == 0 else head_bits + second
        parts.append((begin, part_steps(first + near + far, size)))
        begin += size
    return parts


def peer(name, stride, radix, hop):
    here = lax.axis_index(name)
    digit = lax.rem(here // stride, radix)
    other = lax.rem(digit + hop, radix)
    return digit, other, {name: here + (other - digit) * stride}


def greet(parts):
    kinds = sorted({step[:3] for _, steps in parts for step in steps})
    barrier = pltpu.get_barrier_semaphore()
    count = 0
    for name, stride, radix in kinds:
        for hop in range(1, radix):
            pl.semaphore_signal(
                barrier, inc=1, device_id=peer(name, stride, radix, hop)[2],
                device_id_type=pl.DeviceIdType.MESH,
            )
            count += 1
    pl.semaphore_wait(barrier, count)


def walk(part_at, begin, steps, landings, stages, terms_ref, total, whole, send_sem, recv_sem):
    base, wire = begin, 0
    bases = [begin]

    def copy_to(source, target, device):
        nonlocal wire
        copy = pltpu.make_async_remote_copy(
            src_ref=source, dst_ref=target, send_sem=send_sem.at[part_at, wire], recv_sem=recv_sem.at[part_at, wire],
            device_id=device, device_id_type=pl.DeviceIdType.MESH,
        )
        wire += 1
        copy.start()
        return copy

    for index, (name, stride, radix, halves, size) in enumerate(steps):
        held = terms_ref if index == 0 else total
        copies = []
        for hop in range(1, radix):
            digit, other, device = peer(name, stride, radix, hop)
            give = pl.multiple_of(base + other * size, 16) if halves else base
            landing = landings[index].at[hop - 1]
            if halves and index > 0:
                stage = stages[index].at[hop - 1]
                stage[...] = held[pl.ds(give, size), :].astype(jnp.bfloat16)
                copies.append(copy_to(stage, landing, device))
            else:
                copies.append(copy_to(held.at[pl.ds(give, size), :], landing, device))
        yield
        keep = pl.multiple_of(base + digit * size, 16) if halves else base
        for copy in copies:
            copy.wait()
        value = held[pl.ds(keep, size), :]
        for hop in range(1, radix):
            value = value + landings[index][hop - 1].astype(jnp.float32)
        if index == len(steps) - 1:
            whole[pl.ds(keep, size), :] = value.astype(jnp.bfloat16)
        else:
            total[pl.ds(keep, size), :] = value
        if halves:
            bases.append(keep)
        base = keep
    halving = [step for step in steps if step[3]]
    for index in reversed(range(len(halving))):
        name, stride, radix, _, size = halving[index]
        mine = whole.at[pl.ds(bases[index + 1], size), :]
        copies = [
            copy_to(mine, mine, peer(name, stride, radix, hop)[2]) for hop in range(1, radix)
        ]
        yield
        for copy in copies:
            copy.wait()


def reduce_kernel(parts, layout, terms_ref, after_ref, out_ref, total, whole, send_sem, recv_sem, *bufs):
    greet(parts)
    walks = []
    for at, (begin, steps) in enumerate(parts):
        landings, stages = [[bufs[i] if i is not None else None for i in row] for row in layout[at]]
        walks.append(
            walk(at, begin, steps, landings, stages, terms_ref, total, whole, send_sem, recv_sem)
        )
    while walks:
        walks = [w for w in walks if next(w, 0) is None]
    out_ref[...] = whole[...]


def reduced(terms, after, tiles, heads):
    rows = terms.shape[0]
    parts = plan(tiles, heads, rows)
    bufs, layout, wires = [], [], 0
    for _, steps in parts:
        landings, stages = [], []
        for index, (_, _, radix, halves, size) in enumerate(steps):
            narrow = halves and index > 0
            shape = (radix - 1, size, LANES)
            landings.append(len(bufs))
            bufs.append(pltpu.VMEM(shape, jnp.bfloat16 if narrow else jnp.float32))
            stages.append(len(bufs) if narrow else None)
            if narrow:
                bufs.append(pltpu.VMEM(shape, jnp.bfloat16))
        layout.append((landings, stages))
        wires = max(wires, sum(s[2] - 1 for s in steps) + sum(s[2] - 1 for s in steps if s[3]))
    return pl.pallas_call(
        functools.partial(reduce_kernel, parts, layout),
        out_shape=jax.ShapeDtypeStruct((rows, LANES), jnp.bfloat16),
        in_specs=[VM, pl.BlockSpec(memory_space=pl.ANY)],
        out_specs=VM,
        scratch_shapes=[
            pltpu.VMEM(terms.shape, jnp.float32),
            pltpu.VMEM(terms.shape, jnp.bfloat16),
            pltpu.SemaphoreType.DMA((len(parts), wires)),
            pltpu.SemaphoreType.DMA((len(parts), wires)),
            *bufs,
        ],
        compiler_params=pltpu.CompilerParams(
            collective_id=0, has_side_effects=True, vmem_limit_bytes=VMEM_BYTES
        ),
        cost_estimate=pl.CostEstimate(flops=10**6, bytes_accessed=100 * 10**6, transcendentals=0),
        name="term_sum",
    )(terms, after)


def on_device(feature_map, weight, mask_grad, send_count, send_row, send_col):
    tile_map = feature_map[0]
    height, width, channels = tile_map.shape
    boxes, side = mask_grad.shape[2], mask_grad.shape[3]
    wide = -(-(side + 2) // 16) * 16
    halo = side - 1
    n, cap = send_row.shape[2], send_row.shape[3]
    tiles, heads = lax.axis_size("tile"), lax.axis_size("dp")
    others = max(n - 1, 1)
    below = shifted(tile_map[:halo], "tile", -1)
    me = lax.axis_index("dp").reshape(1)
    slots = jnp.concatenate([send_count.reshape(-1), send_row.reshape(-1), send_col.reshape(-1)])
    room = EDGE + width + 2 * EDGE
    own_shape = jax.ShapeDtypeStruct((cap, side, wide, channels), jnp.bfloat16)
    send_shape = jax.ShapeDtypeStruct((others, cap, side, wide, channels), jnp.bfloat16)
    own, send = pl.pallas_call(
        functools.partial(cut_kernel, n, cap, side, wide),
        out_shape=(own_shape, send_shape),
        in_specs=[SM, SM, VM, VM],
        out_specs=(VM, VM),
        scratch_shapes=[pltpu.VMEM((height + halo, room, channels), jnp.float32)],
        compiler_params=LOCAL,
        name="cut",
    )(me, slots, tile_map, below)

    def swapped(array, sign):
        parts = [rotated(array[k - 1], "dp", sign * k) for k in range(1, n)]
        return jnp.stack(parts) if len(parts) > 1 else parts[0][None]

    got = swapped(send, 1)
    upstream = jnp.pad(mask_grad[0, 0], ((0, 0), (0, 0), (1, wide - side - 1), (0, 0)))
    full = (side + 2) * wide
    rows = 9 * channels * (channels // LANES)
    back_own, back_send, x3, slopes = pl.pallas_call(
        functools.partial(conv_kernel, n, cap, boxes, side, wide),
        out_shape=(
            own_shape,
            send_shape,
            jax.ShapeDtypeStruct((boxes, full, 3 * channels), jnp.bfloat16),
            jax.ShapeDtypeStruct((boxes, side * wide, channels), jnp.bfloat16),
        ),
        in_specs=[SM, VM, VM, VM, VM],
        out_specs=(VM, VM, VM, VM),
        scratch_shapes=[
            pltpu.VMEM((n, cap, side, wide, channels), jnp.bfloat16),
            pltpu.VMEM((full + 2 * EDGE, channels), jnp.float32),
            pltpu.VMEM((boxes, full, 3 * channels), jnp.bfloat16),
            pltpu.VMEM((boxes, side, wide, channels), jnp.bfloat16),
            pltpu.VMEM((boxes, n * cap, 1, channels), jnp.float32),
        ],
        compiler_params=LOCAL,
        name="conv",
    )(me, own, got, weight, upstream)
    back_got = swapped(back_send, -1)
    terms = pl.pallas_call(
        functools.partial(terms_kernel, boxes, side, wide),
        out_shape=jax.ShapeDtypeStruct((rows, LANES), jnp.float32),
        in_specs=[VM, VM],
        out_specs=VM,
        compiler_params=LOCAL,
        cost_estimate=pl.CostEstimate(
            flops=18 * boxes * side * wide * channels * channels, bytes_accessed=6 * 10**6, transcendentals=0
        ),
        name="terms",
    )(x3, slopes)
    main, spill = pl.pallas_call(
        functools.partial(paste_kernel, n, cap, side, wide),
        out_shape=(
            jax.ShapeDtypeStruct((height, width, channels), jnp.float32),
            jax.ShapeDtypeStruct((halo, width, channels), jnp.bfloat16),
        ),
        in_specs=[SM, SM, VM, VM],
        out_specs=(VM, VM),
        scratch_shapes=[pltpu.VMEM((height + halo, room, channels), jnp.float32)],
        compiler_params=LOCAL,
        name="paste",
    )(me, slots, back_own, back_got)
    arriving = shifted(spill, "tile", 1)
    whole = reduced(terms, spill, tiles, heads)
    map_grad = jnp.concatenate([main[:halo] + arriving.astype(jnp.float32), main[halo:]], 0)
    box_total = boxes * tiles * heads
    halves = whole.reshape(channels // LANES, 9 * channels, LANES)
    summed = jnp.concatenate([halves[h] for h in range(channels // LANES)], -1)
    weight_grad = summed.reshape(9, channels, channels).astype(jnp.float32) / box_total
    return (map_grad[None], weight_grad)


def solution(mesh):
    in_specs = (
        P("dp", "tile", None, None),
        P(),
        P("dp", "tile", None, None, None, None),
        P("dp", "tile", None),
        P("dp", "tile", None, None),
        P("dp", "tile", None, None),
    )
    out_specs = (P("dp", "tile", None, None), P())
    return jax.shard_map(
        on_device, mesh=mesh, in_specs=in_specs, out_specs=out_specs, check_vma=False
    )
```

```python
import functools

import jax
import jax.numpy as jnp
from jax import lax
from jax.experimental import pallas as pl
from jax.experimental.pallas import tpu as pltpu
from jax.sharding import PartitionSpec as P

GELU_SCALE = 0.7978845608
GELU_CUBIC = 0.044715
LANES = 128
EDGE = 8
VMEM_BYTES = 40 * 1024 * 1024
VM = pl.BlockSpec(memory_space=pltpu.VMEM)
SM = pl.BlockSpec(memory_space=pltpu.SMEM)
LOCAL = pltpu.CompilerParams(vmem_limit_bytes=VMEM_BYTES)


def shifted(array, axis, by):
    length = lax.axis_size(axis)
    pairs = [(i, i + by) for i in range(length) if 0 <= i + by < length]
    return lax.ppermute(array, axis, pairs)


def rotated(array, axis, by):
    length = lax.axis_size(axis)
    return lax.ppermute(array, axis, [(i, (i + by) % length) for i in range(length)])


def gelu_slope(values):
    inner = GELU_SCALE * (values + GELU_CUBIC * values * values * values)
    tangent = jnp.tanh(inner)
    outer = (
        0.5
        * values
        * (1.0 - tangent * tangent)
        * GELU_SCALE
        * (1.0 + 3.0 * GELU_CUBIC * values * values)
    )
    return 0.5 * (1.0 + tangent) + outer


def cut_kernel(n, cap, side, wide, me_ref, slots_ref, map_ref, below_ref, own_ref, send_ref, ext):
    height, width = map_ref.shape[0], map_ref.shape[1]
    ext[:height, EDGE : EDGE + width, :] = map_ref[...].astype(jnp.float32)
    ext[height:, EDGE : EDGE + width, :] = below_ref[...].astype(jnp.float32)
    me = me_ref[0]
    span = 2 * wide
    cell = lax.broadcasted_iota(jnp.int32, (wide, map_ref.shape[2]), 0)
    inside = (cell >= 1) & (cell <= side)
    for k in range(n):
        head = lax.rem(me + k, n)
        for r in range(cap):
            top, place = slots_ref[n + head * cap + r], slots_ref[n + (n + head) * cap + r] + EDGE - 1
            base = pl.multiple_of(place // 8 * 8, 8)
            back = lax.rem(span - lax.rem(place, 8), span)
            flag = jnp.where(r < slots_ref[head], 1.0, 0.0)
            for y in range(side):
                line = pltpu.roll(ext[top + y, pl.ds(base, span), :], back, 0)[:wide]
                line = jnp.where(inside, line, 0.0)
                if y == 0:
                    line = jnp.where(cell == wide - 1, flag, line)
                line = line.astype(jnp.bfloat16)
                if k == 0:
                    own_ref[r, y] = line
                else:
                    send_ref[k - 1, r, y] = line


def conv_kernel(n, cap, boxes, side, wide, me_ref, own_ref, got_ref, weight_ref, up_ref,
                back_own, back_send, x3, sl, slots, shift, s3, cg, picks):
    channels = weight_ref.shape[2]
    area, full = side * wide, (side + 2) * wide
    me = me_ref[0]
    slots[me] = own_ref[...]
    for k in range(1, n):
        slots[lax.rem(me + n - k, n)] = got_ref[k - 1]
    cell = lax.broadcasted_iota(jnp.int32, (1, wide, channels), 1)
    inside = (cell >= 1) & (cell <= side)
    rank = jnp.zeros((1, channels), jnp.float32)
    for i in range(n):
        for r in range(cap):
            flag = slots[i, r, 0][wide - 1 : wide, :].astype(jnp.float32)
            for b in range(boxes):
                picks[b, i * cap + r] = flag * jnp.where(rank == float(b), 1.0, 0.0)
            rank = rank + flag
    shift[...] = jnp.zeros_like(shift)
    for b in range(boxes):
        box = jnp.zeros((side, wide, channels), jnp.float32)
        for i in range(n):
            for r in range(cap):
                box = box + slots[i, r].astype(jnp.float32) * picks[b, i * cap + r][None]
        box = jnp.where(inside, box, 0.0).reshape(area, channels)
        shift[EDGE + wide : EDGE + wide + area, :] = box
        for t in range(3):
            x3[b, :, t * channels : (t + 1) * channels] = shift[
                EDGE - 1 + t : EDGE - 1 + t + full, :
            ].astype(jnp.bfloat16)
        pre = jnp.zeros((area, channels), jnp.float32)
        for a in range(3):
            pre = pre + jnp.dot(
                x3[b, wide * a : wide * a + area, :],
                weight_ref[3 * a : 3 * a + 3].reshape(3 * channels, channels),
                preferred_element_type=jnp.float32,
            )
        slope = (up_ref[b].reshape(area, channels).astype(jnp.float32) * gelu_slope(pre)).astype(jnp.bfloat16)
        sl[b] = slope
        shift[EDGE + wide : EDGE + wide + area, :] = slope.astype(jnp.float32)
        for t in range(3):
            s3[b, :, t * channels : (t + 1) * channels] = shift[
                EDGE + 1 - t : EDGE + 1 - t + full, :
            ].astype(jnp.bfloat16)
        grad = jnp.zeros((area, channels), jnp.float32)
        for a in range(3):
            for t in range(3):
                grad = grad + lax.dot_general(
                    s3[b, wide * (2 - a) : wide * (2 - a) + area, t * channels : (t + 1) * channels],
                    weight_ref[3 * a + t],
                    (((1,), (1,)), ((), ())),
                    preferred_element_type=jnp.float32,
                )
        grad = jnp.where(inside, grad.reshape(side, wide, channels), 0.0)
        cg[b] = grad.astype(jnp.bfloat16)
    for k in range(n):
        i = lax.rem(me + n - k, n)
        for r in range(cap):
            back = jnp.zeros((side, wide, channels), jnp.float32)
            for b in range(boxes):
                back = back + cg[b].astype(jnp.float32) * picks[b, i * cap + r][None]
            if k == 0:
                back_own[r] = back.astype(jnp.bfloat16)
            else:
                back_send[k - 1, r] = back.astype(jnp.bfloat16)


def terms_kernel(boxes, side, wide, x3, sl, terms_ref):
    channels, area = sl.shape[2], side * wide
    for a in range(3):
        total = jnp.zeros((3 * channels, channels), jnp.float32)
        for b in range(boxes):
            total = total + lax.dot_general(
                x3[b, wide * a : wide * a + area, :], sl[b], (((0,), (0,)), ((), ())),
                preferred_element_type=jnp.float32,
            )
        depth = 3 * channels
        for h in range(channels // LANES):
            start = h * 3 * depth + a * depth
            terms_ref[start : start + depth, :] = total[:, h * LANES : (h + 1) * LANES]


def paste_kernel(n, cap, side, wide, me_ref, slots_ref, own_ref, got_ref, main_ref, spill_ref, canvas):
    height, width = main_ref.shape[0], main_ref.shape[1]
    canvas[...] = jnp.zeros_like(canvas)
    me = me_ref[0]
    for k in range(n):
        head = lax.rem(me + k, n)
        for r in range(cap):

            @pl.when(r < slots_ref[head])
            def _():
                top, place = slots_ref[n + head * cap + r], slots_ref[n + (n + head) * cap + r] + EDGE - 1
                base = pl.multiple_of(place // 8 * 8, 8)
                ahead = lax.rem(place, 8)
                for y in range(side):
                    line = (own_ref[r, y] if k == 0 else got_ref[k - 1, r, y]).astype(jnp.float32)
                    line = jnp.concatenate([line, jnp.zeros_like(line)], 0)
                    window = (top + y, pl.ds(base, 2 * wide), slice(None))
                    canvas[window] = canvas[window] + pltpu.roll(line, ahead, 0)

    main_ref[...] = canvas[:height, EDGE : EDGE + width, :]
    spill_ref[...] = canvas[height:, EDGE : EDGE + width, :].astype(spill_ref.dtype)


def bits_of(name, length):
    return [(name, 1 << i) for i in range(length.bit_length() - 1)]


def part_steps(order, rows):
    steps, size = [], rows
    for name, stride, radix in order:
        if size % (16 * radix) == 0:
            size = size // radix
            steps.append((name, stride, radix, True, size))
        else:
            digits = radix.bit_length() - 1
            steps.extend((name, stride << i, 2, False, size) for i in range(digits))
    return steps


def plan(tiles, heads, rows):
    tile_bits = [(name, bit, 2) for name, bit in bits_of("tile", tiles)]
    head_bits = [(name, bit, 2) for name, bit in bits_of("dp", heads)]
    first, second, far = tile_bits[:1], tile_bits[1:2], tile_bits[2:]
    if len(far) % 2 == 0:
        far = [(name, bit, 4) for name, bit, _ in far[::2]]
    unit = 16 * 32
    parts, begin, pieces = [], 0, 4
    for at in range(pieces):
        size = ((rows // unit) // pieces + (at < (rows // unit) % pieces)) * unit
        near = second + head_bits if at % 2 == 0 else head_bits + second
        parts.append((begin, part_steps(first + near + far, size)))
        begin += size
    return parts


def peer(name, stride, radix, hop):
    here = lax.axis_index(name)
    digit = lax.rem(here // stride, radix)
    other = lax.rem(digit + hop, radix)
    return digit, other, {name: here + (other - digit) * stride}


def greet(parts):
    kinds = sorted({step[:3] for _, steps in parts for step in steps})
    barrier = pltpu.get_barrier_semaphore()
    count = 0
    for name, stride, radix in kinds:
        for hop in range(1, radix):
            pl.semaphore_signal(
                barrier, inc=1, device_id=peer(name, stride, radix, hop)[2],
                device_id_type=pl.DeviceIdType.MESH,
            )
            count += 1
    pl.semaphore_wait(barrier, count)


def send_to(source, target, device, sems, part_at, wire):
    copy = pltpu.make_async_remote_copy(
        src_ref=source, dst_ref=target, send_sem=sems[0].at[part_at, wire], recv_sem=sems[1].at[part_at, wire],
        device_id=device, device_id_type=pl.DeviceIdType.MESH,
    )
    copy.start()
    return copy


def scatter_walk(part_at, begin, steps, landings, stages, terms_ref, total, out_ref, out_at, sems):
    base, wire = begin, 0
    for index, (name, stride, radix, halves, size) in enumerate(steps):
        held = terms_ref if index == 0 else total
        copies = []
        for hop in range(1, radix):
            digit, other, device = peer(name, stride, radix, hop)
            give = pl.multiple_of(base + other * size, 16) if halves else base
            source = held.at[pl.ds(give, size), :]
            if halves and index > 0:
                stages[index][hop - 1] = held[pl.ds(give, size), :].astype(jnp.bfloat16)
                source = stages[index].at[hop - 1]
            copies.append(send_to(source, landings[index].at[hop - 1], device, sems, part_at, wire))
            wire += 1
        yield
        keep = pl.multiple_of(base + digit * size, 16) if halves else base
        for copy in copies:
            copy.wait()
        value = held[pl.ds(keep, size), :]
        for hop in range(1, radix):
            value = value + landings[index][hop - 1].astype(jnp.float32)
        if index == len(steps) - 1:
            out_ref[out_at : out_at + size, :] = value.astype(jnp.bfloat16)
        else:
            total[pl.ds(keep, size), :] = value
        base = keep


def gather_walk(part_at, begin, steps, part_ref, part_row, whole, sems):
    halving = [step for step in steps if step[3]]
    bases, wire = [begin], 0
    for name, stride, radix, _, size in halving:
        bases.append(pl.multiple_of(bases[-1] + peer(name, stride, radix, 1)[0] * size, 16))
    last = halving[-1][4]
    whole[pl.ds(bases[-1], last), :] = part_ref[part_row : part_row + last, :]
    for index in reversed(range(len(halving))):
        name, stride, radix, _, size = halving[index]
        mine = whole.at[pl.ds(bases[index + 1], size), :]
        copies = []
        for hop in range(1, radix):
            copies.append(send_to(mine, mine, peer(name, stride, radix, hop)[2], sems, part_at, wire))
            wire += 1
        yield
        for copy in copies:
            copy.wait()


def part_rows(parts):
    sizes = [steps[-1][4] for _, steps in parts]
    return [sum(sizes[:at]) for at in range(len(sizes) + 1)]


def run(walks):
    while walks:
        walks = [w for w in walks if next(w, 0) is None]


def scatter_kernel(parts, layout, terms_ref, out_ref, total, send_sem, recv_sem, *bufs):
    greet(parts)
    places, walks = part_rows(parts), []
    for at, (begin, steps) in enumerate(parts):
        landings, stages = [[bufs[i] if i is not None else None for i in row] for row in layout[at]]
        walks.append(
            scatter_walk(at, begin, steps, landings, stages, terms_ref, total, out_ref, places[at], (send_sem, recv_sem))
        )
    run(walks)


def gather_kernel(parts, part_ref, after_ref, out_ref, whole, send_sem, recv_sem):
    greet([(begin, [step for step in steps if step[3]]) for begin, steps in parts])
    places = part_rows(parts)
    run([
        gather_walk(at, begin, steps, part_ref, places[at], whole, (send_sem, recv_sem))
        for at, (begin, steps) in enumerate(parts)
    ])
    out_ref[...] = whole[...]


def wire_sems(parts):
    wires = max(sum(step[2] - 1 for step in steps) for _, steps in parts)
    return [pltpu.SemaphoreType.DMA((len(parts), wires)) for _ in range(2)]


def scattered(terms, tiles, heads):
    parts = plan(tiles, heads, terms.shape[0])
    bufs, layout = [], []
    for _, steps in parts:
        landings, stages = [], []
        for index, (_, _, radix, halves, size) in enumerate(steps):
            narrow = halves and index > 0
            shape = (radix - 1, size, LANES)
            landings.append(len(bufs))
            bufs.append(pltpu.VMEM(shape, jnp.bfloat16 if narrow else jnp.float32))
            stages.append(len(bufs) if narrow else None)
            if narrow:
                bufs.append(pltpu.VMEM(shape, jnp.bfloat16))
        layout.append((landings, stages))
    return pl.pallas_call(
        functools.partial(scatter_kernel, parts, layout),
        out_shape=jax.ShapeDtypeStruct((part_rows(parts)[-1], LANES), jnp.bfloat16),
        in_specs=[VM],
        out_specs=VM,
        scratch_shapes=[pltpu.VMEM(terms.shape, jnp.float32), *wire_sems(parts), *bufs],
        compiler_params=pltpu.CompilerParams(
            collective_id=0, has_side_effects=True, vmem_limit_bytes=VMEM_BYTES
        ),
        cost_estimate=pl.CostEstimate(flops=10**6, bytes_accessed=50 * 10**6, transcendentals=0),
        name="term_scatter",
    )(terms)


def gathered(part, after, tiles, heads, rows):
    parts = plan(tiles, heads, rows)
    return pl.pallas_call(
        functools.partial(gather_kernel, parts),
        out_shape=jax.ShapeDtypeStruct((rows, LANES), jnp.bfloat16),
        in_specs=[VM, pl.BlockSpec(memory_space=pl.ANY)],
        out_specs=VM,
        scratch_shapes=[pltpu.VMEM((rows, LANES), jnp.bfloat16), *wire_sems(parts)],
        compiler_params=pltpu.CompilerParams(
            collective_id=1, has_side_effects=True, vmem_limit_bytes=VMEM_BYTES
        ),
        cost_estimate=pl.CostEstimate(flops=10**6, bytes_accessed=50 * 10**6, transcendentals=0),
        name="term_gather",
    )(part, after)


def on_device(feature_map, weight, mask_grad, send_count, send_row, send_col):
    tile_map = feature_map[0]
    height, width, channels = tile_map.shape
    boxes, side = mask_grad.shape[2], mask_grad.shape[3]
    wide = -(-(side + 2) // 16) * 16
    halo = side - 1
    n, cap = send_row.shape[2], send_row.shape[3]
    tiles, heads = lax.axis_size("tile"), lax.axis_size("dp")
    others = max(n - 1, 1)
    below = shifted(tile_map[:halo], "tile", -1)
    me = lax.axis_index("dp").reshape(1)
    slots = jnp.concatenate([send_count.reshape(-1), send_row.reshape(-1), send_col.reshape(-1)])
    room = EDGE + width + 2 * EDGE
    own_shape = jax.ShapeDtypeStruct((cap, side, wide, channels), jnp.bfloat16)
    send_shape = jax.ShapeDtypeStruct((others, cap, side, wide, channels), jnp.bfloat16)
    own, send = pl.pallas_call(
        functools.partial(cut_kernel, n, cap, side, wide),
        out_shape=(own_shape, send_shape),
        in_specs=[SM, SM, VM, VM],
        out_specs=(VM, VM),
        scratch_shapes=[pltpu.VMEM((height + halo, room, channels), jnp.float32)],
        compiler_params=LOCAL,
        name="cut",
    )(me, slots, tile_map, below)

    def swapped(array, sign):
        parts = [rotated(array[k - 1], "dp", sign * k) for k in range(1, n)]
        return jnp.stack(parts) if len(parts) > 1 else parts[0][None]

    got = swapped(send, 1)
    upstream = jnp.pad(mask_grad[0, 0], ((0, 0), (0, 0), (1, wide - side - 1), (0, 0)))
    full = (side + 2) * wide
    rows = 9 * channels * (channels // LANES)
    back_own, back_send, x3, slopes = pl.pallas_call(
        functools.partial(conv_kernel, n, cap, boxes, side, wide),
        out_shape=(
            own_shape,
            send_shape,
            jax.ShapeDtypeStruct((boxes, full, 3 * channels), jnp.bfloat16),
            jax.ShapeDtypeStruct((boxes, side * wide, channels), jnp.bfloat16),
        ),
        in_specs=[SM, VM, VM, VM, VM],
        out_specs=(VM, VM, VM, VM),
        scratch_shapes=[
            pltpu.VMEM((n, cap, side, wide, channels), jnp.bfloat16),
            pltpu.VMEM((full + 2 * EDGE, channels), jnp.float32),
            pltpu.VMEM((boxes, full, 3 * channels), jnp.bfloat16),
            pltpu.VMEM((boxes, side, wide, channels), jnp.bfloat16),
            pltpu.VMEM((boxes, n * cap, 1, channels), jnp.float32),
        ],
        compiler_params=LOCAL,
        name="conv",
    )(me, own, got, weight, upstream)
    back_got = swapped(back_send, -1)
    terms = pl.pallas_call(
        functools.partial(terms_kernel, boxes, side, wide),
        out_shape=jax.ShapeDtypeStruct((rows, LANES), jnp.float32),
        in_specs=[VM, VM],
        out_specs=VM,
        compiler_params=LOCAL,
        cost_estimate=pl.CostEstimate(
            flops=18 * boxes * side * wide * channels * channels, bytes_accessed=6 * 10**6, transcendentals=0
        ),
        name="terms",
    )(x3, slopes)
    part = scattered(terms, tiles, heads)
    main, spill = pl.pallas_call(
        functools.partial(paste_kernel, n, cap, side, wide),
        out_shape=(
            jax.ShapeDtypeStruct((height, width, channels), jnp.float32),
            jax.ShapeDtypeStruct((halo, width, channels), jnp.bfloat16),
        ),
        in_specs=[SM, SM, VM, VM],
        out_specs=(VM, VM),
        scratch_shapes=[pltpu.VMEM((height + halo, room, channels), jnp.float32)],
        compiler_params=LOCAL,
        name="paste",
    )(me, slots, back_own, back_got)
    arriving = shifted(spill, "tile", 1)
    whole = gathered(part, spill, tiles, heads, rows)
    map_grad = jnp.concatenate([main[:halo] + arriving.astype(jnp.float32), main[halo:]], 0)
    box_total = boxes * tiles * heads
    halves = whole.reshape(channels // LANES, 9 * channels, LANES)
    summed = jnp.concatenate([halves[h] for h in range(channels // LANES)], -1)
    weight_grad = summed.reshape(9, channels, channels).astype(jnp.float32) / box_total
    return (map_grad[None], weight_grad)


def solution(mesh):
    in_specs = (
        P("dp", "tile", None, None),
        P(),
        P("dp", "tile", None, None, None, None),
        P("dp", "tile", None),
        P("dp", "tile", None, None),
        P("dp", "tile", None, None),
    )
    out_specs = (P("dp", "tile", None, None), P())
    return jax.shard_map(
        on_device, mesh=mesh, in_specs=in_specs, out_specs=out_specs, check_vma=False
    )
```
